32 devices in a mesh: row: 8 (over z, x), col: 4 (over y, core).
Axes of the slice: x: 2, y: 2, z: 4, core: 2. Of those that a mesh axis runs over, the one named last changes fastest.
Arguments:
- factors: bfloat16 [16384, 256], P(('row', 'col')), may hold values from -1.5 to 1.5
- cores: bfloat16 [8, 256, 256], replicated, may hold values from -0.375 to 0.375
- tiles: bfloat16 [1024, 256, 256], P(('row', 'col')), may hold values from -6 to 6
- tile_coords: int32 [1024, 3], P(('row', 'col')), may hold values from 0 to 15, as said below
- tile_counts: int32 [32], P(('row', 'col')), may hold values from 1 to 32, as said below
Outputs:
- gradient: float32 [16384, 256], P(('row', 'col'))
The draws below stay inside these ranges and needn't reach their ends.
Inputs may be any that keep to these rules, and one draw needn't show every extreme that they name: `tile_coords`: column 0 is a relation below 8, column 1 below 8, column 2 below 16; within one device no two slots have the same three coordinates. `tile_counts`: some device has all 32 slots live.
All inputs are finite; a program needn't handle non-finite values.
Results may differ from the reference program's by a relative error of at most 0.0011.
Values may be sent and summed in bfloat16 or wider, within the bound.
No kernel may reach another device: no remote copies, remote signals or barrier semaphores. Data moves between devices by JAX's collectives and lax.ppermute only.
A program may use at most 128 MiB of HBM per device.

```python
import jax
import jax.numpy as jnp
from jax import lax

RANK = 256
RELS = 8
TILE = 256
BLK = 8
CAP = 32
BLK_COL = 16
NENT = 16384
N_ROW = 8
N_COL = 4
DEVICES = 32


def draw_tile_coords(key, part):
    positions = RELS * BLK * BLK_COL
    keys = jax.random.split(jax.random.fold_in(key, 11), DEVICES)

    def one_device(dev_key):
        return jax.random.permutation(dev_key, positions)[:CAP]
    picked = jax.vmap(one_device)(keys).astype(jnp.int32)
    relation = picked // (BLK * BLK_COL)
    src_index = picked // BLK_COL % BLK
    tgt_index = picked % BLK_COL
    return jnp.stack([relation, src_index, tgt_index], axis=-1).reshape(DEVICES * CAP, 3).astype(jnp.int32)


def draw_tile_counts(key, part):
    key_first = jax.random.fold_in(key, 21)
    key_second = jax.random.fold_in(key, 22)
    key_full = jax.random.fold_in(key, 23)
    first = jax.random.randint(key_first, (DEVICES,), 0, CAP)
    second = jax.random.randint(key_second, (DEVICES,), 0, CAP)
    counts = 1 + jnp.minimum(first, second)
    busiest = jax.random.randint(key_full, (), 0, DEVICES)
    return counts.at[busiest].set(CAP).astype(jnp.int32)


def level_of(rng, extent, shards, smallest, largest):
    def one(dim, shards_of):
        steps = jax.random.uniform(jax.random.fold_in(jax.random.fold_in(rng, 6), dim), (shards_of,), jnp.float32, smallest / len(shards), largest / len(shards))
        return jnp.repeat(jnp.exp(steps), extent[dim] // shards_of).reshape((-1,) + (1,) * (len(extent) - dim - 1))

    level = one(*shards[0])
    for cut in shards[1:]:
        level = level * one(*cut)
    return level


def gaussian(stream_key, extent, scale, bound, cuts=(), kind=jnp.bfloat16):
    factor_of = level_of(stream_key, extent, cuts, -0.22, 0.18) if cuts else 1.0
    drawn = jax.random.normal(stream_key, extent, jnp.float32) * scale * factor_of
    return jnp.minimum(jnp.maximum(drawn, -bound), bound).astype(kind)


def setup_inputs(seed: int = 0) -> dict:
    streams_of = jax.random.split(jax.random.key(seed), 6)
    return {
        "factors": gaussian(streams_of[0], (NENT, RANK), 0.25, 1.5, ((0, 32),)),
        "cores": gaussian(streams_of[1], (RELS, RANK, RANK), RANK ** -0.5, 0.375),
        "tiles": gaussian(streams_of[2], (DEVICES * CAP, TILE, TILE), 1.0, 6.0, ((0, 32),)),
        "tile_coords": draw_tile_coords(jax.random.fold_in(streams_of[5], 71), 0),
        "tile_counts": draw_tile_counts(jax.random.fold_in(streams_of[5], 71), 0),
    }


weight_decay = 1.0


def reference(factors, cores, tiles, tile_coords, tile_counts):
    fac32 = factors.astype(jnp.float32)
    core32 = cores.astype(jnp.float32)
    blocks_all = NENT // TILE
    left_core = jnp.einsum('nr,krs->kns', fac32, core32).astype(jnp.bfloat16).reshape(RELS, blocks_all, TILE, RANK)
    right_core = jnp.einsum('nr,ksr->kns', fac32, core32).astype(jnp.bfloat16).reshape(RELS, blocks_all, TILE, RANK)
    fac_blocks = factors.reshape(blocks_all, TILE, RANK)

    def device_pass(device, grads):
        row_pos = device // N_COL
        col_pos = device % N_COL
        live_count = tile_counts[device]

        def group_pass(group, grads):
            start = (device * CAP + group * 8).astype(jnp.int32)
            coords = lax.dynamic_slice_in_dim(tile_coords, start, 8, 0)
            values = lax.dynamic_slice_in_dim(tiles, start, 8, 0).astype(jnp.float32)
            is_live = (group * 8 + jnp.arange(8, dtype=jnp.int32)) < live_count
            relation = coords[:, 0]
            src_block = row_pos * BLK + coords[:, 1]
            tgt_block = col_pos * BLK_COL + coords[:, 2]
            left = left_core[relation, src_block].astype(jnp.float32)
            right = fac_blocks[tgt_block].astype(jnp.float32)
            right_rel = right_core[relation, tgt_block].astype(jnp.float32)
            predicted = jnp.einsum('gtr,gur->gtu', left, right)
            resid_half = jnp.where(is_live[:, None, None], values - predicted, 0.0).astype(jnp.bfloat16)
            resid = lax.optimization_barrier(resid_half).astype(jnp.float32)
            src_grad = jnp.einsum('gtu,gur->gtr', resid, right_rel)
            tgt_grad = jnp.einsum('gtu,gtr->gur', resid, left)
            return grads.at[src_block].add(src_grad).at[tgt_block].add(tgt_grad)

        return lax.fori_loop(0, (live_count + 7) // 8, group_pass, grads)

    grads = jnp.zeros((blocks_all, TILE, RANK), jnp.float32)
    grads = lax.fori_loop(0, N_ROW * N_COL, device_pass, grads)
    return weight_decay * fac32 - grads.reshape(NENT, RANK) / TILE
```

```python
import functools

import jax
import jax.numpy as jnp
from jax import lax
from jax.experimental import pallas as pl
from jax.experimental.pallas import tpu as pltpu
from jax.sharding import Mesh
from jax.sharding import PartitionSpec as P

weight_decay = 1.0
AXES = ("zz", "xx", "col")
UNROLL = 4
CONTRACT_LAST = (((1,), (1,)), ((), ()))
CONTRACT_FIRST = (((0,), (0,)), ((), ()))


def dot(a, b, dims=(((1,), (0,)), ((), ()))):
    return lax.dot_general(a, b, dims, preferred_element_type=jnp.float32)


def slots_kernel(n_col, ratio, scalars, coords, cores_ref, *refs):
    n_src, n_tgt = n_col, n_col * ratio
    src_refs, refs = refs[:n_src], refs[n_src:]
    tgt_refs, refs = refs[:n_tgt], refs[n_tgt:]
    tiles_ref, gt_out, keep_out, send_out = refs[:4]
    src, tgt, tile_buf, gs_acc, gt_acc, tile_sems, sems = refs[4:]
    cap, tile = tile_buf.shape[0], tile_buf.shape[1]
    rows = src_refs[0].shape[0]
    plane, x_pos, col_pos, live = scalars[0], scalars[1], scalars[2], scalars[3]

    for s in range(cap):
        pltpu.make_async_copy(tiles_ref.at[s], tile_buf.at[s], tile_sems.at[s]).start()
    copies = []
    for o in range(n_src):
        at = pl.multiple_of((col_pos ^ o) * rows, rows)
        copies.append(pltpu.make_async_copy(src_refs[o], src.at[pl.ds(at, rows)], sems.at[o]))
    for d in range(n_col):
        for s in range(ratio):
            part = lax.rem(x_pos + (ratio - s), ratio) * n_col + (plane ^ d)
            at = pl.multiple_of(part * rows, rows)
            index = d * ratio + s
            copies.append(
                pltpu.make_async_copy(tgt_refs[index], tgt.at[pl.ds(at, rows)], sems.at[n_src + index])
            )
    for copy in copies:
        copy.start()
    gs_acc[...] = jnp.zeros_like(gs_acc)
    gt_acc[...] = jnp.zeros_like(gt_acc)
    for copy in copies:
        copy.wait()
    for s in range(cap):
        pltpu.make_async_copy(tiles_ref.at[s], tile_buf.at[s], tile_sems.at[s]).wait()

    def group(g, carry):
        work = []
        for u in range(UNROLL):
            s = g * UNROLL + u
            k = coords[3 * s]
            a_at = pl.ds(pl.multiple_of(coords[3 * s + 1] * tile, tile), tile)
            b_at = pl.ds(pl.multiple_of(coords[3 * s + 2] * tile, tile), tile)
            core = cores_ref[k]
            right = tgt[b_at]
            left = dot(src[a_at], core).astype(jnp.bfloat16)
            right_rel = dot(right, core, CONTRACT_LAST).astype(jnp.bfloat16)
            predicted = dot(left, right, CONTRACT_LAST)
            resid = jnp.where(s < live, tile_buf[s].astype(jnp.float32) - predicted, 0.0)
            resid = resid.astype(jnp.bfloat16)
            work.append((a_at, b_at, dot(resid, right_rel), dot(resid, left, CONTRACT_FIRST)))
        for a_at, b_at, src_grad, tgt_grad in work:
            gs_acc[a_at] += src_grad
            gt_acc[b_at] += tgt_grad
        return carry

    lax.fori_loop(0, (live + UNROLL - 1) // UNROLL, group, 0)
    gt_out[...] = gt_acc[...].astype(gt_out.dtype)
    bit = col_pos & 1
    for h in range(n_col // 2):
        at = pl.multiple_of((2 * h + bit) * rows, rows)
        keep_out[h] = gs_acc[pl.ds(at, rows)]
        at = pl.multiple_of((2 * h + 1 - bit) * rows, rows)
        send_out[h] = gs_acc[pl.ds(at, rows)]


def swap(value, bit, n_col):
    return lax.ppermute(value, "col", [(i, i ^ bit) for i in range(n_col)])


def local(factors, cores, tiles, tile_coords, tile_counts):
    planes = lax.axis_size("zz")
    ratio = lax.axis_size("xx")
    n_col = lax.axis_size("col")
    rows, rank = factors.shape
    cap, tile = tiles.shape[0], tiles.shape[1]
    plane, x_pos, col_pos = lax.axis_index("zz"), lax.axis_index("xx"), lax.axis_index("col")

    tgt_parts = []
    for d in range(n_col):
        pairs = [
            ((p * ratio + x) * n_col + q, ((q ^ d) * ratio + x) * n_col + p)
            for p in range(planes)
            for x in range(ratio)
            for q in range(n_col)
        ]
        tgt_parts.append(lax.ppermute(factors, AXES, pairs))
    src_parts = {0: factors}
    bit = n_col // 2
    while bit:
        for o, value in list(src_parts.items()):
            src_parts[o | bit] = swap(value, bit, n_col)
        bit //= 2
    tgt_all = []
    for d in range(n_col):
        tgt_all.append(tgt_parts[d])
        for s in range(1, ratio):
            pairs = [(x, (x + s) % ratio) for x in range(ratio)]
            tgt_all.append(lax.ppermute(tgt_parts[d], "xx", pairs))

    scalars = jnp.stack([plane, x_pos, col_pos, tile_counts[0]]).astype(jnp.int32)
    src_rows, tgt_rows = n_col * rows, n_col * ratio * rows
    any_spec = pl.BlockSpec(memory_space=pl.ANY)
    vmem_spec = pl.BlockSpec(memory_space=pltpu.VMEM)
    smem_spec = pl.BlockSpec(memory_space=pltpu.SMEM)
    n_parts = n_col + n_col * ratio
    half = jax.ShapeDtypeStruct((n_col // 2, rows, rank), jnp.float32)
    tgt_grad, src_keep, src_send = pl.pallas_call(
        functools.partial(slots_kernel, n_col, ratio),
        out_shape=[jax.ShapeDtypeStruct((tgt_rows, rank), jnp.bfloat16), half, half],
        in_specs=[smem_spec, smem_spec, vmem_spec] + [any_spec] * (n_parts + 1),
        out_specs=[vmem_spec] * 3,
        scratch_shapes=[
            pltpu.VMEM((src_rows, rank), factors.dtype),
            pltpu.VMEM((tgt_rows, rank), factors.dtype),
            pltpu.VMEM(tiles.shape, tiles.dtype),
            pltpu.VMEM((src_rows, rank), jnp.float32),
            pltpu.VMEM((tgt_rows, rank), jnp.float32),
            pltpu.SemaphoreType.DMA((cap,)),
            pltpu.SemaphoreType.DMA((n_parts,)),
        ],
        compiler_params=pltpu.CompilerParams(vmem_limit_bytes=40 * 2**20),
        cost_estimate=pl.CostEstimate(
            flops=cap * 5 * 2 * tile**3, bytes_accessed=16 * 2**20, transcendentals=0
        ),
    )(scalars, tile_coords.reshape(-1), cores, *[src_parts[o] for o in range(n_col)], *tgt_all, tiles)

    recv = swap(src_send, 1, n_col)
    arrived = lax.all_to_all(tgt_grad, ("xx", "col"), 0, 0, tiled=True)
    src_sum = src_keep + recv
    bit = 2
    while bit < n_col:
        pairs = src_sum.reshape(src_sum.shape[0] // 2, 2, rows, rank)
        mine = (col_pos // bit) % 2
        out = lax.dynamic_index_in_dim(pairs, 1 - mine, 1, keepdims=False).astype(jnp.bfloat16)
        kept = lax.dynamic_index_in_dim(pairs, mine, 1, keepdims=False)
        src_sum = kept + swap(out, bit, n_col).astype(jnp.float32)
        bit *= 2
    summed = arrived.reshape(ratio, n_col, rows, rank).astype(jnp.float32).sum(0).astype(jnp.bfloat16)
    landed = lax.all_to_all(summed.reshape(n_col * rows, rank), "zz", 0, 0, tiled=True)
    tgt_sum = landed.reshape(planes, rows, rank).astype(jnp.float32).sum(0)
    return weight_decay * factors.astype(jnp.float32) - (src_sum[0] + tgt_sum) / tile


def solution(mesh):
    n_row, n_col = mesh.shape["row"], mesh.shape["col"]
    split = Mesh(mesh.devices.reshape(n_col, n_row // n_col, n_col), AXES)
    in_specs = (P(AXES, None), P(), P(AXES, None, None), P(AXES, None), P(AXES))
    return jax.shard_map(local, mesh=split, in_specs=in_specs, out_specs=P(AXES, None), check_vma=False)
```

```python
import functools

import jax
import jax.numpy as jnp
from jax import lax
from jax.experimental import pallas as pl
from jax.experimental.pallas import tpu as pltpu
from jax.sharding import Mesh
from jax.sharding import PartitionSpec as P

weight_decay = 1.0
AXES = ("zz", "xx", "col")
UNROLL = 8
CONTRACT_LAST = (((1,), (1,)), ((), ()))
CONTRACT_FIRST = (((0,), (0,)), ((), ()))


def dot(a, b, dims=(((1,), (0,)), ((), ()))):
    return lax.dot_general(a, b, dims, preferred_element_type=jnp.float32)


def mirror(value, size):
    out, bit = 0, 1
    while bit < size:
        out = out * 2 + (value // bit) % 2
        bit *= 2
    return out


def slots_kernel(first, last, n_col, ratio, scalars, coords, cores_hbm, *refs):
    n_x = last - first
    opens, closes = first == 0, last == ratio
    src_refs, refs = refs[:n_col], refs[n_col:]
    tgt_refs, refs = refs[: n_col * n_x], refs[n_col * n_x :]
    tiles_hbm, refs = refs[0], refs[1:]
    if not opens:
        gs_in, refs = refs[0], refs[2:]
    gt_out, refs = refs[0], refs[1:]
    gs_outs, refs = (refs[:2], refs[2:]) if closes else (refs[:1], refs[1:])
    cores, src, tgt, tiles, resids, left, right, gs_acc, gt_acc, slot_of, tgt_of, sems = refs
    cap, tile = tiles.shape[0], tiles.shape[1]
    rows = src_refs[0].shape[0]
    block = n_col * rows
    plane, x_pos, col_pos, live = scalars[0], scalars[1], scalars[2], scalars[3]

    copies = [pltpu.make_async_copy(cores_hbm, cores, sems.at[0])]
    for o in range(n_col):
        at = pl.multiple_of((col_pos ^ o) * rows, rows)
        copies.append(pltpu.make_async_copy(src_refs[o], src.at[pl.ds(at, rows)], sems.at[1 + o]))
    for d in range(n_col):
        part = mirror(plane ^ col_pos ^ d, n_col)
        for n in range(n_x):
            at = pl.multiple_of((n * n_col + part) * rows, rows)
            index = d * n_x + n
            copies.append(
                pltpu.make_async_copy(tgt_refs[index], tgt.at[pl.ds(at, rows)], sems.at[1 + n_col + index])
            )
    if not opens:
        copies.append(pltpu.make_async_copy(gs_in, gs_acc, sems.at[1 + n_col * (n_x + 1)]))
    tiles_copy = pltpu.make_async_copy(tiles_hbm, tiles, sems.at[2 + n_col * (n_x + 1)])
    for copy in copies:
        copy.start()
    tiles_copy.start()
    if opens:
        gs_acc[...] = jnp.zeros_like(gs_acc)
    gt_acc[...] = jnp.zeros_like(gt_acc)

    def choose(s, count):
        b = coords[3 * s + 2]
        step = lax.rem(x_pos - b // (block // tile) + ratio, ratio)
        taken = (step >= first) & (step < last)
        slot_of[count] = s
        tgt_of[count] = (step - first) * (block // tile) + lax.rem(b, block // tile)
        return count + taken.astype(jnp.int32)

    count = lax.fori_loop(0, live, choose, 0)
    for u in range(UNROLL):
        slot_of[count + u] = 0
        tgt_of[count + u] = 0
    groups = (count + UNROLL - 1) // UNROLL
    for copy in copies:
        copy.wait()

    def place(index):
        return pl.ds(pl.multiple_of(index * tile, tile), tile)

    def products(g, carry):
        for u in range(UNROLL):
            i = g * UNROLL + u
            s = slot_of[i]
            core = cores[coords[3 * s]]
            left[i] = dot(src[place(coords[3 * s + 1])], core).astype(jnp.bfloat16)
            right[i] = dot(tgt[place(tgt_of[i])], core, CONTRACT_LAST).astype(jnp.bfloat16)
        return carry

    def residuals(g, carry):
        for u in range(UNROLL):
            i = g * UNROLL + u
            s = slot_of[i]
            predicted = dot(left[i], tgt[place(tgt_of[i])], CONTRACT_LAST)
            resid = jnp.where(i < count, tiles[s].astype(jnp.float32) - predicted, 0.0)
            resids[i] = resid.astype(jnp.bfloat16)
        return carry

    def gradients(g, carry):
        for u in range(UNROLL):
            i = g * UNROLL + u
            resid = resids[i]
            gs_acc[place(coords[3 * slot_of[i] + 1])] += dot(resid, right[i])
            gt_acc[place(tgt_of[i])] += dot(resid, left[i], CONTRACT_FIRST)
        return carry

    lax.fori_loop(0, groups, products, 0)
    tiles_copy.wait()
    lax.fori_loop(0, groups, residuals, 0)
    lax.fori_loop(0, groups, gradients, 0)

    outs = []
    if closes:
        for h in range(n_col // 2):
            for n in range(2):
                at = pl.multiple_of((2 * h + ((col_pos + n) & 1)) * rows, rows)
                outs.append((gs_acc.at[pl.ds(at, rows)], gs_outs[n].at[h]))
    else:
        outs.append((gs_acc, gs_outs[0]))
    outs = [pltpu.make_async_copy(a, b, sems.at[i]) for i, (a, b) in enumerate(outs)]
    for copy in outs:
        copy.start()
    tgt[...] = gt_acc[...].astype(tgt.dtype)
    used = len(outs)
    for n in range(n_x):
        x_of = lax.rem(x_pos + (ratio - first - n), ratio)
        outs.append(pltpu.make_async_copy(tgt.at[pl.ds(n * block, block)], gt_out.at[x_of], sems.at[used + n]))
        outs[-1].start()
    for copy in outs:
        copy.wait()


def run_slots(first, last, n_col, ratio, scalars, coords, cores, src_parts, tgt_parts, tiles, carried):
    rows, rank = src_parts[0].shape
    cap, tile = tiles.shape[0], tiles.shape[1]
    n_x, block = last - first, n_col * rows
    any_spec = pl.BlockSpec(memory_space=pl.ANY)
    smem_spec = pl.BlockSpec(memory_space=pltpu.SMEM)
    gt = jax.ShapeDtypeStruct((ratio, block, rank), jnp.bfloat16)
    if last == ratio:
        half = jax.ShapeDtypeStruct((n_col // 2, rows, rank), jnp.float32)
        gs = [half, half]
    else:
        gs = [jax.ShapeDtypeStruct((block, rank), jnp.float32)]
    operands = [scalars, coords, cores, *src_parts, *tgt_parts, tiles, *carried]
    return pl.pallas_call(
        functools.partial(slots_kernel, first, last, n_col, ratio),
        out_shape=[gt, *gs],
        in_specs=[smem_spec, smem_spec] + [any_spec] * (len(operands) - 2),
        out_specs=[any_spec] * (1 + len(gs)),
        input_output_aliases={len(operands) - 1: 0} if carried else {},
        scratch_shapes=[
            pltpu.VMEM(cores.shape, cores.dtype),
            pltpu.VMEM((block, rank), jnp.bfloat16),
            pltpu.VMEM((n_x * block, rank), jnp.bfloat16),
            pltpu.VMEM((cap, tile, tile), jnp.bfloat16),
            pltpu.VMEM((cap, tile, tile), jnp.bfloat16),
            pltpu.VMEM((cap, tile, rank), jnp.bfloat16),
            pltpu.VMEM((cap, tile, rank), jnp.bfloat16),
            pltpu.VMEM((block, rank), jnp.float32),
            pltpu.VMEM((n_x * block, rank), jnp.float32),
            pltpu.SMEM((cap + UNROLL,), jnp.int32),
            pltpu.SMEM((cap + UNROLL,), jnp.int32),
            pltpu.SemaphoreType.DMA((n_col * (n_x + 1) + 3,)),
        ],
        compiler_params=pltpu.CompilerParams(vmem_limit_bytes=56 * 2**20),
        cost_estimate=pl.CostEstimate(
            flops=cap * 5 * 2 * tile**3 // ratio, bytes_accessed=12 * 2**20, transcendentals=0
        ),
    )(*operands)


def swap(value, bit, n_col):
    return lax.ppermute(value, "col", [(i, i ^ bit) for i in range(n_col)])


def local(factors, cores, tiles, tile_coords, tile_counts):
    planes = lax.axis_size("zz")
    ratio = lax.axis_size("xx")
    n_col = lax.axis_size("col")
    rows, rank = factors.shape
    tile = tiles.shape[1]
    plane, x_pos, col_pos = lax.axis_index("zz"), lax.axis_index("xx"), lax.axis_index("col")
    scalars = jnp.stack([plane, x_pos, col_pos, tile_counts[0]]).astype(jnp.int32)
    coords = tile_coords.reshape(-1)

    own = []
    for d in range(n_col):
        pairs = [
            ((p * ratio + x) * n_col + q, ((mirror(q, n_col) ^ p ^ d) * ratio + x) * n_col + p)
            for p in range(planes)
            for x in range(ratio)
            for q in range(n_col)
        ]
        own.append(lax.ppermute(factors, AXES, pairs))
    src = {0: factors}
    bit = n_col // 2
    while bit:
        for o, value in list(src.items()):
            src[o | bit] = swap(value, bit, n_col)
        bit //= 2
    src = [src[o] for o in range(n_col)]
    cross = [
        lax.ppermute(own[d], "xx", [(x, (x + s) % ratio) for x in range(ratio)])
        for d in range(n_col)
        for s in range(1, ratio)
    ]

    fixed = (n_col, ratio, scalars, coords, cores, src)
    done = run_slots(0, 1, *fixed, own, tiles, [])
    if ratio > 1:
        done = run_slots(1, ratio, *fixed, cross, tiles, [done[1], done[0]])
    tgt_grad, src_keep, src_send = done

    recv = swap(src_send, 1, n_col)
    arrived = lax.all_to_all(tgt_grad.reshape(-1, rank), ("xx", "col"), 0, 0, tiled=True)
    src_sum = src_keep + recv
    bit = 2
    while bit < n_col:
        pairs = src_sum.reshape(src_sum.shape[0] // 2, 2, rows, rank)
        mine = (col_pos // bit) % 2
        out = lax.dynamic_index_in_dim(pairs, 1 - mine, 1, keepdims=False).astype(jnp.bfloat16)
        kept = lax.dynamic_index_in_dim(pairs, mine, 1, keepdims=False)
        src_sum = kept + swap(out, bit, n_col).astype(jnp.float32)
        bit *= 2
    arrived = arrived.reshape(ratio, n_col * rows, rank)
    summed = sum(arrived[s].astype(jnp.float32) for s in range(ratio)).astype(jnp.bfloat16)
    landed = lax.all_to_all(summed, "zz", 0, 0, tiled=True).reshape(planes, rows, rank)
    tgt_sum = sum(landed[p].astype(jnp.float32) for p in range(planes))
    return weight_decay * factors.astype(jnp.float32) - (src_sum[0] + tgt_sum) / tile


def solution(mesh):
    n_row, n_col = mesh.shape["row"], mesh.shape["col"]
    split = Mesh(mesh.devices.reshape(n_col, n_row // n_col, n_col), AXES)
    in_specs = (P(AXES, None), P(), P(AXES, None, None), P(AXES, None), P(AXES))
    return jax.shard_map(local, mesh=split, in_specs=in_specs, out_specs=P(AXES, None), check_vma=False)
```

```python
import functools

import jax
import jax.numpy as jnp
from jax import lax
from jax.experimental import pallas as pl
from jax.experimental.pallas import tpu as pltpu
from jax.sharding import Mesh
from jax.sharding import PartitionSpec as P

weight_decay = 1.0
AXES = ("zz", "xx", "col")
UNROLL = 8
VMEM_LIMIT = 56 * 2**20
COST = 0
CONTRACT_LAST = (((1,), (1,)), ((), ()))
CONTRACT_FIRST = (((0,), (0,)), ((), ()))


def dot(a, b, dims=(((1,), (0,)), ((), ()))):
    return lax.dot_general(a, b, dims, preferred_element_type=jnp.float32)


def mirror(value, size):
    out, bit = 0, 1
    while bit < size:
        out = out * 2 + (value // bit) % 2
        bit *= 2
    return out


def slots_kernel(first, last, late, n_wait, n_col, ratio, scalars, coords, cores_hbm, *refs):
    n_x = last - first
    opens, closes = first == 0, last == ratio and late != 1
    parts = [d for d in range(n_col) if late is None or d // 2 % 2 == late]
    src_refs, refs = refs[:n_col], refs[n_col:]
    tgt_refs, refs = refs[: len(parts) * n_x], refs[len(parts) * n_x :]
    tiles_hbm, refs = refs[0], refs[1:]
    if not opens:
        gs_in, refs = refs[0], refs[1:]
    refs = refs[n_wait:]
    gt_outs, refs = refs[: len(parts) * n_x], refs[len(parts) * n_x :]
    gs_outs, refs = (refs[:2], refs[2:]) if closes else (refs[:1], refs[1:])
    cores, src, tgt, tiles, resids, left, right, gs_acc, gt_acc, slot_of, tgt_of, tile_sems, sems = refs
    cap, tile = tiles.shape[0], tiles.shape[1]
    rows = src_refs[0].shape[0]
    src_tiles = n_col * rows // tile
    plane, x_pos, col_pos, live = scalars[0], scalars[1], scalars[2], scalars[3]

    def part_at(d, n):
        place = n * n_col + mirror(plane ^ col_pos ^ d, n_col)
        return pl.ds(pl.multiple_of(place * rows, rows), rows)

    copies = [pltpu.make_async_copy(cores_hbm, cores, sems.at[0])]
    for o in range(n_col):
        at = pl.multiple_of((col_pos ^ o) * rows, rows)
        copies.append(pltpu.make_async_copy(src_refs[o], src.at[pl.ds(at, rows)], sems.at[1 + o]))
    for i, d in enumerate(parts):
        for n in range(n_x):
            index = i * n_x + n
            copies.append(
                pltpu.make_async_copy(tgt_refs[index], tgt.at[part_at(d, n)], sems.at[1 + n_col + index])
            )
    for copy in copies:
        copy.start()
    if not opens:
        gs_copy = pltpu.make_async_copy(gs_in, gs_acc, sems.at[1 + n_col + len(parts) * n_x])
        gs_copy.start()

    def choose(s, count):
        b = coords[2, s]
        step = lax.rem(x_pos - b // src_tiles + ratio, ratio)
        place = lax.rem(b, src_tiles)
        taken = (step >= first) & (step < last)
        if late is not None:
            part = mirror(place * tile // rows, n_col) ^ plane ^ col_pos
            taken = taken & ((part // 2) % 2 == late)
        slot_of[count] = s
        tgt_of[count] = (step - first) * src_tiles + place

        @pl.when(taken)
        def _():
            pltpu.make_async_copy(tiles_hbm.at[s], tiles.at[count], tile_sems.at[count]).start()

        return count + taken.astype(jnp.int32)

    count = lax.fori_loop(0, live, choose, 0)
    for u in range(UNROLL):
        slot_of[count + u] = 0
        tgt_of[count + u] = 0
    groups = (count + UNROLL - 1) // UNROLL
    if opens:
        gs_acc[...] = jnp.zeros_like(gs_acc)
    gt_acc[...] = jnp.zeros_like(gt_acc)
    for copy in copies:
        copy.wait()

    def place(index):
        return pl.ds(pl.multiple_of(index * tile, tile), tile)

    def products(g, carry):
        for u in range(UNROLL):
            i = g * UNROLL + u
            s = slot_of[i]
            core = cores[coords[0, s]]
            left[i] = dot(src[place(coords[1, s])], core).astype(jnp.bfloat16)
            right[i] = dot(tgt[place(tgt_of[i])], core, CONTRACT_LAST).astype(jnp.bfloat16)
        return carry

    def residuals(g, carry):
        for u in range(UNROLL):
            i = g * UNROLL + u
            predicted = dot(left[i], tgt[place(tgt_of[i])], CONTRACT_LAST)
            resid = jnp.where(i < count, tiles[i].astype(jnp.float32) - predicted, 0.0)
            resids[i] = resid.astype(jnp.bfloat16)
        return carry

    def gradients(g, carry):
        for u in range(UNROLL):
            i = g * UNROLL + u
            resid = resids[i]
            gs_acc[place(coords[1, slot_of[i]])] += dot(resid, right[i])
            gt_acc[place(tgt_of[i])] += dot(resid, left[i], CONTRACT_FIRST)
        return carry

    def arrive(i, carry):
        pltpu.make_async_copy(tiles_hbm.at[slot_of[i]], tiles.at[i], tile_sems.at[i]).wait()
        return carry

    lax.fori_loop(0, groups, products, 0)
    lax.fori_loop(0, count, arrive, 0)
    lax.fori_loop(0, groups, residuals, 0)
    if not opens:
        gs_copy.wait()
    lax.fori_loop(0, groups, gradients, 0)

    outs = []
    if closes:
        for h in range(n_col // 2):
            for n in range(2):
                at = pl.multiple_of((2 * h + ((col_pos + n) & 1)) * rows, rows)
                outs.append((gs_acc.at[pl.ds(at, rows)], gs_outs[n].at[h]))
    else:
        outs.append((gs_acc, gs_outs[0]))
    outs = [pltpu.make_async_copy(a, b, sems.at[i]) for i, (a, b) in enumerate(outs)]
    for copy in outs:
        copy.start()
    for i, d in enumerate(parts):
        for n in range(n_x):
            tgt[part_at(d, n)] = gt_acc[part_at(d, n)].astype(tgt.dtype)
            copy = pltpu.make_async_copy(tgt.at[part_at(d, n)], gt_outs[i * n_x + n], sems.at[len(outs)])
            copy.start()
            outs.append(copy)
    for copy in outs:
        copy.wait()


def run_slots(
    first, last, late, n_col, ratio, scalars, coords, cores, src_parts, tgt_parts, tiles, carried, wait=()
):
    rows, rank = src_parts[0].shape
    cap, tile = tiles.shape[0], tiles.shape[1]
    n_x, block = last - first, n_col * rows
    any_spec = pl.BlockSpec(memory_space=pl.ANY)
    smem_spec = pl.BlockSpec(memory_space=pltpu.SMEM)
    n_out = len(tgt_parts)
    outs = [jax.ShapeDtypeStruct((rows, rank), jnp.bfloat16)] * n_out
    if last == ratio and late != 1:
        outs += [jax.ShapeDtypeStruct((n_col // 2, rows, rank), jnp.float32)] * 2
    else:
        outs += [jax.ShapeDtypeStruct((block, rank), jnp.float32)]
    operands = [scalars, coords, cores, *src_parts, *tgt_parts, tiles, *carried, *wait]
    outs = pl.pallas_call(
        functools.partial(slots_kernel, first, last, late, len(wait), n_col, ratio),
        out_shape=outs,
        in_specs=[smem_spec, smem_spec] + [any_spec] * (len(operands) - 2),
        out_specs=[any_spec] * len(outs),
        scratch_shapes=[
            pltpu.VMEM(cores.shape, cores.dtype),
            pltpu.VMEM((block, rank), jnp.bfloat16),
            pltpu.VMEM((n_x * block, rank), jnp.bfloat16),
            pltpu.VMEM((cap, tile, tile), jnp.bfloat16),
            pltpu.VMEM((cap, tile, tile), jnp.bfloat16),
            pltpu.VMEM((cap, tile, rank), jnp.bfloat16),
            pltpu.VMEM((cap, tile, rank), jnp.bfloat16),
            pltpu.VMEM((block, rank), jnp.float32),
            pltpu.VMEM((n_x * block, rank), jnp.float32),
            pltpu.SMEM((cap + UNROLL,), jnp.int32),
            pltpu.SMEM((cap + UNROLL,), jnp.int32),
            pltpu.SemaphoreType.DMA((cap,)),
            pltpu.SemaphoreType.DMA((2 * n_col * (n_x + 1) + 2,)),
        ],
        compiler_params=pltpu.CompilerParams(vmem_limit_bytes=VMEM_LIMIT),
        cost_estimate=pl.CostEstimate(flops=COST, bytes_accessed=COST, transcendentals=0),
    )(*operands)
    return outs[:n_out], outs[n_out:]


def swap(value, bit, n_col):
    return lax.ppermute(value, "col", [(i, i ^ bit) for i in range(n_col)])


def local(factors, cores, tiles, tile_coords, tile_counts):
    planes = lax.axis_size("zz")
    ratio = lax.axis_size("xx")
    n_col = lax.axis_size("col")
    rows, rank = factors.shape
    tile = tiles.shape[1]
    plane, x_pos, col_pos = lax.axis_index("zz"), lax.axis_index("xx"), lax.axis_index("col")
    scalars = jnp.stack([plane, x_pos, col_pos, tile_counts[0]]).astype(jnp.int32)
    coords = tile_coords.T

    def part_pairs(d, target):
        spots = [(p, x, j) for p in range(planes) for x in range(ratio) for j in range(n_col)]
        at = lambda p, x, j: (p * ratio + x) * n_col + j
        return [(at(p, x, j), at(*target(p, x, j, mirror(p ^ j ^ d, n_col)))) for p, x, j in spots]

    own = {}
    for d in [*range(1, n_col, 2), *range(0, n_col, 2)]:
        pairs = part_pairs(d, lambda p, x, j, q: (j, x, q))
        own[d] = lax.ppermute(factors, AXES, [(b, a) for a, b in pairs])
    src = {0: factors}
    bit = n_col // 2
    while bit:
        for o, value in list(src.items()):
            src[o | bit] = swap(value, bit, n_col)
        bit //= 2
    src = [src[o] for o in range(n_col)]
    cross = {
        d: [lax.ppermute(own[d], "xx", [(x, (x + s) % ratio) for x in range(ratio)]) for s in range(1, ratio)]
        for d in own
    }

    fixed = (n_col, ratio, scalars, coords, cores, src)
    own_grad, src_grad = run_slots(0, 1, None, *fixed, [own[d] for d in range(n_col)], tiles, [])
    grads = {d: [own_grad[d]] for d in range(n_col)}
    if ratio > 1:
        held = [v for d in range(n_col) for v in cross[d]]
        target, src_grad = run_slots(1, ratio, None, *fixed, held, tiles, src_grad)
        for d in range(n_col):
            grads[d].extend(target[d * (ratio - 1) : (d + 1) * (ratio - 1)])
    src_keep, src_send = src_grad

    for d in range(0, n_col, 4):
        gone = [lax.ppermute(v, "zz", [(p, p ^ 1) for p in range(planes)]) for v in grads.pop(d + 1)]
        grads[d] = [
            (a.astype(jnp.float32) + b.astype(jnp.float32)).astype(jnp.bfloat16) for a, b in zip(grads[d], gone)
        ]
    src_sum = src_keep + swap(src_send, 1, n_col)
    bit = 2
    while bit < n_col:
        pairs = src_sum.reshape(src_sum.shape[0] // 2, 2, rows, rank)
        mine = (col_pos // bit) % 2
        out = lax.dynamic_index_in_dim(pairs, 1 - mine, 1, keepdims=False).astype(jnp.bfloat16)
        kept = lax.dynamic_index_in_dim(pairs, mine, 1, keepdims=False)
        src_sum = kept + swap(out, bit, n_col).astype(jnp.float32)
        bit *= 2
    total = src_sum[0]
    for d in sorted(grads, key=lambda d: -(d // 2 % 2)):
        arrived = [
            lax.ppermute(grads[d][t], AXES, part_pairs(d, lambda p, x, j, q, t=t: (p, (x - t) % ratio, q)))
            for t in range(ratio)
        ]
        term = sum(v.astype(jnp.float32) for v in arrived).astype(jnp.bfloat16)
        pairs = [
            ((p * ratio + x) * n_col + q, ((p ^ mirror(q, n_col) ^ d) * ratio + x) * n_col + q)
            for p in range(planes)
            for x in range(ratio)
            for q in range(n_col)
        ]
        total = total + lax.ppermute(term, AXES, pairs).astype(jnp.float32)
    return weight_decay * factors.astype(jnp.float32) - total / tile


def solution(mesh):
    n_row, n_col = mesh.shape["row"], mesh.shape["col"]
    split = Mesh(mesh.devices.reshape(n_col, n_row // n_col, n_col), AXES)
    in_specs = (P(AXES, None), P(), P(AXES, None, None), P(AXES, None), P(AXES))
    return jax.shard_map(local, mesh=split, in_specs=in_specs, out_specs=P(AXES, None), check_vma=False)
```

```python
import functools

import jax
import jax.numpy as jnp
from jax import lax
from jax.experimental import pallas as pl
from jax.experimental.pallas import tpu as pltpu
from jax.sharding import Mesh
from jax.sharding import PartitionSpec as P

weight_decay = 1.0
AXES = ("zz", "xx", "col")
UNROLL = 8
VMEM_LIMIT = 56 * 2**20
COST = 0
CONTRACT_LAST = (((1,), (1,)), ((), ()))
CONTRACT_FIRST = (((0,), (0,)), ((), ()))


def dot(a, b, dims=(((1,), (0,)), ((), ()))):
    return lax.dot_general(a, b, dims, preferred_element_type=jnp.float32)


def mirror(value, size):
    out, bit = 0, 1
    while bit < size:
        out = out * 2 + (value // bit) % 2
        bit *= 2
    return out


def slots_kernel(first, last, late, n_wait, n_col, ratio, scalars, coords, cores_hbm, *refs):
    n_x = last - first
    opens, closes = first == 0, last == ratio and late != 1
    parts = [d for d in range(n_col) if late is None or d // 2 % 2 == late]
    src_refs, refs = refs[:n_col], refs[n_col:]
    tgt_refs, refs = refs[: len(parts) * n_x], refs[len(parts) * n_x :]
    tiles_hbm, refs = refs[0], refs[1:]
    if not opens:
        gs_in, refs = refs[0], refs[1:]
    refs = refs[n_wait:]
    gt_outs, refs = refs[: len(parts) * n_x], refs[len(parts) * n_x :]
    gs_outs, refs = (refs[:2], refs[2:]) if closes else (refs[:1], refs[1:])
    cores, src, tgt, tiles, resids, left, right, gs_acc, gt_acc, slot_of, tgt_of, tile_sems, sems = refs
    cap, tile = tiles.shape[0], tiles.shape[1]
    rows = src_refs[0].shape[0]
    src_tiles = n_col * rows // tile
    plane, x_pos, col_pos, live = scalars[0], scalars[1], scalars[2], scalars[3]

    def part_at(d, n):
        place = n * n_col + mirror(plane ^ col_pos ^ d, n_col)
        return pl.ds(pl.multiple_of(place * rows, rows), rows)

    copies = [pltpu.make_async_copy(cores_hbm, cores, sems.at[0])]
    for o in range(n_col):
        at = pl.multiple_of((col_pos ^ o) * rows, rows)
        copies.append(pltpu.make_async_copy(src_refs[o], src.at[pl.ds(at, rows)], sems.at[1 + o]))
    for i, d in enumerate(parts):
        for n in range(n_x):
            index = i * n_x + n
            copies.append(
                pltpu.make_async_copy(tgt_refs[index], tgt.at[part_at(d, n)], sems.at[1 + n_col + index])
            )
    for copy in copies:
        copy.start()
    if not opens:
        gs_copy = pltpu.make_async_copy(gs_in, gs_acc, sems.at[1 + n_col + len(parts) * n_x])
        gs_copy.start()

    def choose(s, count):
        b = coords[2, s]
        step = lax.rem(x_pos - b // src_tiles + ratio, ratio)
        place = lax.rem(b, src_tiles)
        taken = (step >= first) & (step < last)
        if late is not None:
            part = mirror(place * tile // rows, n_col) ^ plane ^ col_pos
            taken = taken & ((part // 2) % 2 == late)
        slot_of[count] = s
        tgt_of[count] = (step - first) * src_tiles + place

        @pl.when(taken)
        def _():
            pltpu.make_async_copy(tiles_hbm.at[s], tiles.at[count], tile_sems.at[count]).start()

        return count + taken.astype(jnp.int32)

    count = lax.fori_loop(0, live, choose, 0)
    for u in range(UNROLL):
        slot_of[count + u] = 0
        tgt_of[count + u] = 0
    groups = (count + UNROLL - 1) // UNROLL
    if opens:
        gs_acc[...] = jnp.zeros_like(gs_acc)
    gt_acc[...] = jnp.zeros_like(gt_acc)
    for copy in copies:
        copy.wait()

    def place(index):
        return pl.ds(pl.multiple_of(index * tile, tile), tile)

    def products(g, carry):
        for u in range(UNROLL):
            i = g * UNROLL + u
            s = slot_of[i]
            core = cores[coords[0, s]]
            left[i] = dot(src[place(coords[1, s])], core).astype(jnp.bfloat16)
            right[i] = dot(tgt[place(tgt_of[i])], core, CONTRACT_LAST).astype(jnp.bfloat16)
        return carry

    def residuals(g, carry):
        for u in range(UNROLL):
            i = g * UNROLL + u
            predicted = dot(left[i], tgt[place(tgt_of[i])], CONTRACT_LAST)
            resid = jnp.where(i < count, tiles[i].astype(jnp.float32) - predicted, 0.0)
            resids[i] = resid.astype(jnp.bfloat16)
        return carry

    def gradients(g, carry):
        for u in range(UNROLL):
            i = g * UNROLL + u
            resid = resids[i]
            gs_acc[place(coords[1, slot_of[i]])] += dot(resid, right[i])
            gt_acc[place(tgt_of[i])] += dot(resid, left[i], CONTRACT_FIRST)
        return carry

    def arrive(i, carry):
        pltpu.make_async_copy(tiles_hbm.at[slot_of[i]], tiles.at[i], tile_sems.at[i]).wait()
        return carry

    lax.fori_loop(0, groups, products, 0)
    lax.fori_loop(0, count, arrive, 0)
    lax.fori_loop(0, groups, residuals, 0)
    if not opens:
        gs_copy.wait()
    lax.fori_loop(0, groups, gradients, 0)

    outs = []
    if closes:
        for h in range(n_col // 2):
            for n in range(2):
                at = pl.multiple_of((2 * h + ((col_pos + n) & 1)) * rows, rows)
                outs.append((gs_acc.at[pl.ds(at, rows)], gs_outs[n].at[h]))
    else:
        outs.append((gs_acc, gs_outs[0]))
    outs = [pltpu.make_async_copy(a, b, sems.at[i]) for i, (a, b) in enumerate(outs)]
    for copy in outs:
        copy.start()
    for i, d in enumerate(parts):
        for n in range(n_x):
            tgt[part_at(d, n)] = gt_acc[part_at(d, n)].astype(tgt.dtype)
            copy = pltpu.make_async_copy(tgt.at[part_at(d, n)], gt_outs[i * n_x + n], sems.at[len(outs)])
            copy.start()
            outs.append(copy)
    for copy in outs:
        copy.wait()


def run_slots(
    first, last, late, n_col, ratio, scalars, coords, cores, src_parts, tgt_parts, tiles, carried, wait=()
):
    rows, rank = src_parts[0].shape
    cap, tile = tiles.shape[0], tiles.shape[1]
    n_x, block = last - first, n_col * rows
    any_spec = pl.BlockSpec(memory_space=pl.ANY)
    smem_spec = pl.BlockSpec(memory_space=pltpu.SMEM)
    n_out = len(tgt_parts)
    outs = [jax.ShapeDtypeStruct((rows, rank), jnp.bfloat16)] * n_out
    if last == ratio and late != 1:
        outs += [jax.ShapeDtypeStruct((n_col // 2, rows, rank), jnp.float32)] * 2
    else:
        outs += [jax.ShapeDtypeStruct((block, rank), jnp.float32)]
    operands = [scalars, coords, cores, *src_parts, *tgt_parts, tiles, *carried, *wait]
    outs = pl.pallas_call(
        functools.partial(slots_kernel, first, last, late, len(wait), n_col, ratio),
        out_shape=outs,
        in_specs=[smem_spec, smem_spec] + [any_spec] * (len(operands) - 2),
        out_specs=[any_spec] * len(outs),
        scratch_shapes=[
            pltpu.VMEM(cores.shape, cores.dtype),
            pltpu.VMEM((block, rank), jnp.bfloat16),
            pltpu.VMEM((n_x * block, rank), jnp.bfloat16),
            pltpu.VMEM((cap, tile, tile), jnp.bfloat16),
            pltpu.VMEM((cap, tile, tile), jnp.bfloat16),
            pltpu.VMEM((cap, tile, rank), jnp.bfloat16),
            pltpu.VMEM((cap, tile, rank), jnp.bfloat16),
            pltpu.VMEM((block, rank), jnp.float32),
            pltpu.VMEM((n_x * block, rank), jnp.float32),
            pltpu.SMEM((cap + UNROLL,), jnp.int32),
            pltpu.SMEM((cap + UNROLL,), jnp.int32),
            pltpu.SemaphoreType.DMA((cap,)),
            pltpu.SemaphoreType.DMA((2 * n_col * (n_x + 1) + 2,)),
        ],
        compiler_params=pltpu.CompilerParams(vmem_limit_bytes=VMEM_LIMIT),
        cost_estimate=pl.CostEstimate(flops=COST, bytes_accessed=COST, transcendentals=0),
    )(*operands)
    return outs[:n_out], outs[n_out:]


def swap(value, bit, n_col):
    return lax.ppermute(value, "col", [(i, i ^ bit) for i in range(n_col)])


def local(factors, cores, tiles, tile_coords, tile_counts):
    planes = lax.axis_size("zz")
    ratio = lax.axis_size("xx")
    n_col = lax.axis_size("col")
    rows, rank = factors.shape
    tile = tiles.shape[1]
    plane, x_pos, col_pos = lax.axis_index("zz"), lax.axis_index("xx"), lax.axis_index("col")
    scalars = jnp.stack([plane, x_pos, col_pos, tile_counts[0]]).astype(jnp.int32)
    coords = tile_coords.T

    def part_pairs(d, target):
        spots = [(p, x, j) for p in range(planes) for x in range(ratio) for j in range(n_col)]
        at = lambda p, x, j: (p * ratio + x) * n_col + j
        return [(at(p, x, j), at(*target(p, x, j, mirror(p ^ j ^ d, n_col)))) for p, x, j in spots]

    own = {}
    for d in [*range(1, n_col, 2), *range(0, n_col, 2)]:
        pairs = part_pairs(d, lambda p, x, j, q: (j, x, q))
        own[d] = lax.ppermute(factors, AXES, [(b, a) for a, b in pairs])
    src = {0: factors}
    bit = n_col // 2
    while bit:
        for o, value in list(src.items()):
            if bit == 1 and o:
                value = lax.optimization_barrier((value, own[0]))[0]
            src[o | bit] = swap(value, bit, n_col)
        bit //= 2
    src = [src[o] for o in range(n_col)]
    cross = {
        d: [lax.ppermute(own[d], "xx", [(x, (x + s) % ratio) for x in range(ratio)]) for s in range(1, ratio)]
        for d in range(n_col)
    }

    fixed = (n_col, ratio, scalars, coords, cores, src)
    def to_owner(value, d, t):
        return lax.ppermute(value, AXES, part_pairs(d, lambda p, x, j, q: (p, (x - t) % ratio, q)))

    def to_pair(value):
        return lax.ppermute(value, "zz", [(p, p ^ 1) for p in range(planes)])

    halving = [d for d in range(n_col) if d // 2 % 2 == 1]
    direct = [d for d in range(n_col) if d // 2 % 2 == 0]
    own_grad, src_grad = run_slots(0, 1, None, *fixed, [own[d] for d in range(n_col)], tiles, [])
    came = {d: [to_pair(own_grad[d + 1])] for d in halving[::2]}
    arrived = {d: [to_owner(own_grad[d], d, 0)] for d in direct}
    grads = {d: [own_grad[d]] for d in range(n_col)}
    if ratio > 1:
        held = [v for d in range(n_col) for v in cross[d]]
        target, src_grad = run_slots(1, ratio, None, *fixed, held, tiles, src_grad, own_grad)
        target = {d: target[d * (ratio - 1) : (d + 1) * (ratio - 1)] for d in range(n_col)}
        target, came, arrived = lax.optimization_barrier((target, came, arrived))
        for d in range(n_col):
            grads[d].extend(target[d])
        for t in range(1, ratio):
            for d in came:
                came[d].append(to_pair(grads[d + 1][t]))
            for d in direct:
                arrived[d].append(to_owner(grads[d][t], d, t))
    src_keep, src_send = src_grad

    src_sum = src_keep + swap(src_send, 1, n_col)
    bit = 2
    while bit < n_col:
        pairs = src_sum.reshape(src_sum.shape[0] // 2, 2, rows, rank)
        mine = (col_pos // bit) % 2
        out = lax.dynamic_index_in_dim(pairs, 1 - mine, 1, keepdims=False).astype(jnp.bfloat16)
        kept = lax.dynamic_index_in_dim(pairs, mine, 1, keepdims=False)
        src_sum = kept + swap(out, bit, n_col).astype(jnp.float32)
        bit *= 2
    total = src_sum[0]

    for d in came:
        arrived[d] = [
            to_owner((a.astype(jnp.float32) + b.astype(jnp.float32)).astype(jnp.bfloat16), d, t)
            for t, (a, b) in enumerate(zip(grads[d], came[d]))
        ]
    landed = []
    for d, values in arrived.items():
        term = sum(v.astype(jnp.float32) for v in values).astype(jnp.bfloat16)
        pairs = [
            ((p * ratio + x) * n_col + q, ((p ^ mirror(q, n_col) ^ d) * ratio + x) * n_col + q)
            for p in range(planes)
            for x in range(ratio)
            for q in range(n_col)
        ]
        landed.append(lax.ppermute(term, AXES, pairs))
    total = total + sum(v.astype(jnp.float32) for v in landed)
    return weight_decay * factors.astype(jnp.float32) - total / tile


def solution(mesh):
    n_row, n_col = mesh.shape["row"], mesh.shape["col"]
    split = Mesh(mesh.devices.reshape(n_col, n_row // n_col, n_col), AXES)
    in_specs = (P(AXES, None), P(), P(AXES, None, None), P(AXES, None), P(AXES))
    return jax.shard_map(local, mesh=split, in_specs=in_specs, out_specs=P(AXES, None), check_vma=False)
```

```python
import functools

import jax
import jax.numpy as jnp
from jax import lax
from jax.experimental import pallas as pl
from jax.experimental.pallas import tpu as pltpu
from jax.sharding import Mesh
from jax.sharding import PartitionSpec as P

weight_decay = 1.0
AXES = ("zz", "xx", "col")
UNROLL = 8
VMEM_LIMIT = 56 * 2**20
COST = 0
CONTRACT_LAST = (((1,), (1,)), ((), ()))
CONTRACT_FIRST = (((0,), (0,)), ((), ()))


def dot(a, b, dims=(((1,), (0,)), ((), ()))):
    return lax.dot_general(a, b, dims, preferred_element_type=jnp.float32)


def mirror(value, size):
    out, bit = 0, 1
    while bit < size:
        out = out * 2 + (value // bit) % 2
        bit *= 2
    return out


def slots_kernel(first, last, n_col, ratio, scalars, coords, cores_hbm, *refs):
    n_x = last - first
    opens, closes = first == 0, last == ratio
    parts = [*range(n_col)]
    src_refs, refs = refs[:n_col], refs[n_col:]
    tgt_refs, refs = refs[: len(parts) * n_x], refs[len(parts) * n_x :]
    tiles_hbm, refs = refs[0], refs[1:]
    if not opens:
        gs_in, refs = refs[0], refs[1:]
    gt_outs, refs = refs[: len(parts) * n_x], refs[len(parts) * n_x :]
    gs_outs, refs = (refs[:2], refs[2:]) if closes else (refs[:1], refs[1:])
    cores, src, tgt, tiles, resids, left, right, gs_acc, gt_acc, slot_of, tgt_of, tile_sems, sems = refs
    cap, tile = tiles.shape[0], tiles.shape[1]
    rows = src_refs[0].shape[0]
    src_tiles = n_col * rows // tile
    plane, x_pos, col_pos, live = scalars[0], scalars[1], scalars[2], scalars[3]

    def part_at(d, n):
        place = n * n_col + mirror(plane ^ col_pos ^ d, n_col)
        return pl.ds(pl.multiple_of(place * rows, rows), rows)

    copies = [pltpu.make_async_copy(cores_hbm, cores, sems.at[0])]
    for o in range(n_col):
        at = pl.multiple_of((col_pos ^ o) * rows, rows)
        copies.append(pltpu.make_async_copy(src_refs[o], src.at[pl.ds(at, rows)], sems.at[1 + o]))
    for i, d in enumerate(parts):
        for n in range(n_x):
            index = i * n_x + n
            copies.append(
                pltpu.make_async_copy(tgt_refs[index], tgt.at[part_at(d, n)], sems.at[1 + n_col + index])
            )
    for copy in copies:
        copy.start()
    if not opens:
        gs_copy = pltpu.make_async_copy(gs_in, gs_acc, sems.at[1 + n_col + len(parts) * n_x])
        gs_copy.start()

    def choose(s, count):
        b = coords[2, s]
        step = lax.rem(x_pos - b // src_tiles + ratio, ratio)
        place = lax.rem(b, src_tiles)
        taken = (step >= first) & (step < last)
        slot_of[count] = s
        tgt_of[count] = (step - first) * src_tiles + place

        @pl.when(taken)
        def _():
            pltpu.make_async_copy(tiles_hbm.at[s], tiles.at[count], tile_sems.at[count]).start()

        return count + taken.astype(jnp.int32)

    count = lax.fori_loop(0, live, choose, 0)
    for u in range(UNROLL):
        slot_of[count + u] = 0
        tgt_of[count + u] = 0
    groups = (count + UNROLL - 1) // UNROLL
    if opens:
        gs_acc[...] = jnp.zeros_like(gs_acc)
    gt_acc[...] = jnp.zeros_like(gt_acc)
    for copy in copies:
        copy.wait()

    def place(index):
        return pl.ds(pl.multiple_of(index * tile, tile), tile)

    def products(g, carry):
        for u in range(UNROLL):
            i = g * UNROLL + u
            s = slot_of[i]
            core = cores[coords[0, s]]
            left[i] = dot(src[place(coords[1, s])], core).astype(jnp.bfloat16)
            right[i] = dot(tgt[place(tgt_of[i])], core, CONTRACT_LAST).astype(jnp.bfloat16)
        return carry

    def residuals(g, carry):
        for u in range(UNROLL):
            i = g * UNROLL + u
            predicted = dot(left[i], tgt[place(tgt_of[i])], CONTRACT_LAST)
            resid = jnp.where(i < count, tiles[i].astype(jnp.float32) - predicted, 0.0)
            resids[i] = resid.astype(jnp.bfloat16)
        return carry

    def gradients(g, carry):
        for u in range(UNROLL):
            i = g * UNROLL + u
            resid = resids[i]
            gs_acc[place(coords[1, slot_of[i]])] += dot(resid, right[i])
            gt_acc[place(tgt_of[i])] += dot(resid, left[i], CONTRACT_FIRST)
        return carry

    def arrive(i, carry):
        pltpu.make_async_copy(tiles_hbm.at[slot_of[i]], tiles.at[i], tile_sems.at[i]).wait()
        return carry

    lax.fori_loop(0, groups, products, 0)
    lax.fori_loop(0, count, arrive, 0)
    lax.fori_loop(0, groups, residuals, 0)
    if not opens:
        gs_copy.wait()
    lax.fori_loop(0, groups, gradients, 0)

    outs = []
    if closes:
        for h in range(n_col // 2):
            for n in range(2):
                at = pl.multiple_of((2 * h + ((col_pos + n) & 1)) * rows, rows)
                outs.append((gs_acc.at[pl.ds(at, rows)], gs_outs[n].at[h]))
    else:
        outs.append((gs_acc, gs_outs[0]))
    outs = [pltpu.make_async_copy(a, b, sems.at[i]) for i, (a, b) in enumerate(outs)]
    for copy in outs:
        copy.start()
    for i, d in enumerate(parts):
        for n in range(n_x):
            tgt[part_at(d, n)] = gt_acc[part_at(d, n)].astype(tgt.dtype)
            copy = pltpu.make_async_copy(tgt.at[part_at(d, n)], gt_outs[i * n_x + n], sems.at[len(outs)])
            copy.start()
            outs.append(copy)
    for copy in outs:
        copy.wait()


def run_slots(
    first, last, n_col, ratio, scalars, coords, cores, src_parts, tgt_parts, tiles, carried
):
    rows, rank = src_parts[0].shape
    cap, tile = tiles.shape[0], tiles.shape[1]
    n_x, block = last - first, n_col * rows
    any_spec = pl.BlockSpec(memory_space=pl.ANY)
    smem_spec = pl.BlockSpec(memory_space=pltpu.SMEM)
    n_out = len(tgt_parts)
    outs = [jax.ShapeDtypeStruct((rows, rank), jnp.bfloat16)] * n_out
    if last == ratio:
        outs += [jax.ShapeDtypeStruct((n_col // 2, rows, rank), jnp.float32)] * 2
    else:
        outs += [jax.ShapeDtypeStruct((block, rank), jnp.float32)]
    operands = [scalars, coords, cores, *src_parts, *tgt_parts, tiles, *carried]
    outs = pl.pallas_call(
        functools.partial(slots_kernel, first, last, n_col, ratio),
        out_shape=outs,
        in_specs=[smem_spec, smem_spec] + [any_spec] * (len(operands) - 2),
        out_specs=[any_spec] * len(outs),
        scratch_shapes=[
            pltpu.VMEM(cores.shape, cores.dtype),
            pltpu.VMEM((block, rank), jnp.bfloat16),
            pltpu.VMEM((n_x * block, rank), jnp.bfloat16),
            pltpu.VMEM((cap, tile, tile), jnp.bfloat16),
            pltpu.VMEM((cap, tile, tile), jnp.bfloat16),
            pltpu.VMEM((cap, tile, rank), jnp.bfloat16),
            pltpu.VMEM((cap, tile, rank), jnp.bfloat16),
            pltpu.VMEM((block, rank), jnp.float32),
            pltpu.VMEM((n_x * block, rank), jnp.float32),
            pltpu.SMEM((cap + UNROLL,), jnp.int32),
            pltpu.SMEM((cap + UNROLL,), jnp.int32),
            pltpu.SemaphoreType.DMA((cap,)),
            pltpu.SemaphoreType.DMA((2 * n_col * (n_x + 1) + 2,)),
        ],
        compiler_params=pltpu.CompilerParams(vmem_limit_bytes=VMEM_LIMIT),
        cost_estimate=pl.CostEstimate(flops=COST, bytes_accessed=COST, transcendentals=0),
    )(*operands)
    return outs[:n_out], outs[n_out:]


def swap(value, bit, n_col):
    return lax.ppermute(value, "col", [(i, i ^ bit) for i in range(n_col)])


def local(factors, cores, tiles, tile_coords, tile_counts):
    planes = lax.axis_size("zz")
    ratio = lax.axis_size("xx")
    n_col = lax.axis_size("col")
    rows, rank = factors.shape
    tile = tiles.shape[1]
    plane, x_pos, col_pos = lax.axis_index("zz"), lax.axis_index("xx"), lax.axis_index("col")
    scalars = jnp.stack([plane, x_pos, col_pos, tile_counts[0]]).astype(jnp.int32)
    coords = tile_coords.T

    def part_pairs(d, target):
        spots = [(p, x, j) for p in range(planes) for x in range(ratio) for j in range(n_col)]
        at = lambda p, x, j: (p * ratio + x) * n_col + j
        return [(at(p, x, j), at(*target(p, x, j, mirror(p ^ j ^ d, n_col)))) for p, x, j in spots]

    own = {}
    for d in [*range(1, n_col, 2), *range(0, n_col, 2)]:
        pairs = part_pairs(d, lambda p, x, j, q: (j, x, q))
        own[d] = lax.ppermute(factors, AXES, [(b, a) for a, b in pairs])
    src = {0: factors}
    bit = n_col // 2
    while bit:
        for o, value in list(src.items()):
            if bit == 1 and o:
                value = lax.optimization_barrier((value, own[0]))[0]
            src[o | bit] = swap(value, bit, n_col)
        bit //= 2
    src = [src[o] for o in range(n_col)]
    cross = {
        d: [lax.ppermute(own[d], "xx", [(x, (x + s) % ratio) for x in range(ratio)]) for s in range(1, ratio)]
        for d in range(n_col)
    }

    fixed = (n_col, ratio, scalars, coords, cores, src)
    def to_owner(value, d, t):
        return lax.ppermute(value, AXES, part_pairs(d, lambda p, x, j, q: (p, (x - t) % ratio, q)))

    def to_pair(value):
        return lax.ppermute(value, "zz", [(p, p ^ 1) for p in range(planes)])

    halving = [d for d in range(n_col) if d // 2 % 2 == 1]
    direct = [d for d in range(n_col) if d // 2 % 2 == 0]
    own_grad, src_grad = run_slots(0, 1, *fixed, [own[d] for d in range(n_col)], tiles, [])
    came = {d: [to_pair(own_grad[d + 1])] for d in halving[::2]}
    arrived = {d: [to_owner(own_grad[d], d, 0)] for d in direct}
    grads = {d: [own_grad[d]] for d in range(n_col)}
    if ratio > 1:
        held = [v for d in range(n_col) for v in cross[d]]
        target, src_grad = run_slots(1, ratio, *fixed, held, tiles, src_grad)
        target = {d: target[d * (ratio - 1) : (d + 1) * (ratio - 1)] for d in range(n_col)}
        target, came, arrived = lax.optimization_barrier((target, came, arrived))
        for d in range(n_col):
            grads[d].extend(target[d])
        for t in range(1, ratio):
            for d in came:
                came[d].append(to_pair(grads[d + 1][t]))
            for d in direct:
                arrived[d].append(to_owner(grads[d][t], d, t))
    src_keep, src_send = src_grad

    src_sum = src_keep + swap(src_send, 1, n_col)
    bit = 2
    while bit < n_col:
        pairs = src_sum.reshape(src_sum.shape[0] // 2, 2, rows, rank)
        mine = (col_pos // bit) % 2
        out = lax.dynamic_index_in_dim(pairs, 1 - mine, 1, keepdims=False).astype(jnp.bfloat16)
        kept = lax.dynamic_index_in_dim(pairs, mine, 1, keepdims=False)
        src_sum = kept + swap(out, bit, n_col).astype(jnp.float32)
        bit *= 2
    total = src_sum[0]

    for d in came:
        arrived[d] = [
            to_owner((a.astype(jnp.float32) + b.astype(jnp.float32)).astype(jnp.bfloat16), d, t)
            for t, (a, b) in enumerate(zip(grads[d], came[d]))
        ]
    landed = []
    for d, values in arrived.items():
        term = sum(v.astype(jnp.float32) for v in values).astype(jnp.bfloat16)
        pairs = [
            ((p * ratio + x) * n_col + q, ((p ^ mirror(q, n_col) ^ d) * ratio + x) * n_col + q)
            for p in range(planes)
            for x in range(ratio)
            for q in range(n_col)
        ]
        landed.append(lax.ppermute(term, AXES, pairs))
    total = total + sum(v.astype(jnp.float32) for v in landed)
    return weight_decay * factors.astype(jnp.float32) - total / tile


def solution(mesh):
    n_row, n_col = mesh.shape["row"], mesh.shape["col"]
    split = Mesh(mesh.devices.reshape(n_col, n_row // n_col, n_col), AXES)
    in_specs = (P(AXES, None), P(), P(AXES, None, None), P(AXES, None), P(AXES))
    return jax.shard_map(local, mesh=split, in_specs=in_specs, out_specs=P(AXES, None), check_vma=False)
```

```python
import functools

import jax
import jax.numpy as jnp
from jax import lax
from jax.experimental import pallas as pl
from jax.experimental.pallas import tpu as pltpu
from jax.sharding import Mesh
from jax.sharding import PartitionSpec as P

weight_decay = 1.0
AXES = ("zz", "xx", "col")
UNROLL = 8
VMEM_LIMIT = 56 * 2**20
COST = 0
CONTRACT_LAST = (((1,), (1,)), ((), ()))
CONTRACT_FIRST = (((0,), (0,)), ((), ()))


def dot(a, b, dims=(((1,), (0,)), ((), ()))):
    return lax.dot_general(a, b, dims, preferred_element_type=jnp.float32)


def mirror(value, size):
    out, bit = 0, 1
    while bit < size:
        out = out * 2 + (value // bit) % 2
        bit *= 2
    return out


def slots_kernel(first, last, n_col, ratio, scalars, coords, cores_hbm, *refs):
    n_x = last - first
    opens, closes = first == 0, last == ratio
    parts = [*range(n_col)]
    src_refs, refs = refs[:n_col], refs[n_col:]
    tgt_refs, refs = refs[: len(parts) * n_x], refs[len(parts) * n_x :]
    tiles_hbm, refs = refs[0], refs[1:]
    if not opens:
        gs_in, refs = refs[0], refs[1:]
    gt_outs, refs = refs[: len(parts) * n_x], refs[len(parts) * n_x :]
    gs_outs, refs = (refs[:2], refs[2:]) if closes else (refs[:1], refs[1:])
    cores, src, tgt, tiles, resids, left, right, gs_acc, gt_acc, slot_of, tgt_of, tile_sems, sems = refs
    cap, tile = tiles.shape[0], tiles.shape[1]
    rows = src_refs[0].shape[0]
    src_tiles = n_col * rows // tile
    plane, x_pos, col_pos, live = scalars[0], scalars[1], scalars[2], scalars[3]

    def part_at(d, n):
        place = n * n_col + mirror(plane ^ col_pos ^ d, n_col)
        return pl.ds(pl.multiple_of(place * rows, rows), rows)

    copies = [pltpu.make_async_copy(cores_hbm, cores, sems.at[0])]
    for o in range(n_col):
        at = pl.multiple_of((col_pos ^ o) * rows, rows)
        copies.append(pltpu.make_async_copy(src_refs[o], src.at[pl.ds(at, rows)], sems.at[1 + o]))
    for i, d in enumerate(parts):
        for n in range(n_x):
            index = i * n_x + n
            copies.append(
                pltpu.make_async_copy(tgt_refs[index], tgt.at[part_at(d, n)], sems.at[1 + n_col + index])
            )
    for copy in copies:
        copy.start()
    if not opens:
        gs_copy = pltpu.make_async_copy(gs_in, gs_acc, sems.at[1 + n_col + len(parts) * n_x])
        gs_copy.start()

    def choose(s, count):
        b = coords[2, s]
        step = lax.rem(x_pos - b // src_tiles + ratio, ratio)
        place = lax.rem(b, src_tiles)
        taken = (step >= first) & (step < last)
        slot_of[count] = s
        tgt_of[count] = (step - first) * src_tiles + place

        @pl.when(taken)
        def _():
            pltpu.make_async_copy(tiles_hbm.at[s], tiles.at[count], tile_sems.at[count]).start()

        return count + taken.astype(jnp.int32)

    count = lax.fori_loop(0, live, choose, 0)
    for u in range(UNROLL):
        slot_of[count + u] = 0
        tgt_of[count + u] = 0
    groups = (count + UNROLL - 1) // UNROLL
    if opens:
        gs_acc[...] = jnp.zeros_like(gs_acc)
    gt_acc[...] = jnp.zeros_like(gt_acc)
    for copy in copies:
        copy.wait()

    def place(index):
        return pl.ds(pl.multiple_of(index * tile, tile), tile)

    def products(g, carry):
        for u in range(UNROLL):
            i = g * UNROLL + u
            s = slot_of[i]
            core = cores[coords[0, s]]
            left[i] = dot(src[place(coords[1, s])], core).astype(jnp.bfloat16)
            right[i] = dot(tgt[place(tgt_of[i])], core, CONTRACT_LAST).astype(jnp.bfloat16)
        return carry

    def residuals(g, carry):
        for u in range(UNROLL):
            i = g * UNROLL + u
            predicted = dot(left[i], tgt[place(tgt_of[i])], CONTRACT_LAST)
            resid = jnp.where(i < count, tiles[i].astype(jnp.float32) - predicted, 0.0)
            resids[i] = resid.astype(jnp.bfloat16)
        return carry

    def gradients(g, carry):
        for u in range(UNROLL):
            i = g * UNROLL + u
            resid = resids[i]
            gs_acc[place(coords[1, slot_of[i]])] += dot(resid, right[i])
            gt_acc[place(tgt_of[i])] += dot(resid, left[i], CONTRACT_FIRST)
        return carry

    def arrive(i, carry):
        pltpu.make_async_copy(tiles_hbm.at[slot_of[i]], tiles.at[i], tile_sems.at[i]).wait()
        return carry

    lax.fori_loop(0, groups, products, 0)
    lax.fori_loop(0, count, arrive, 0)
    lax.fori_loop(0, groups, residuals, 0)
    if not opens:
        gs_copy.wait()
    lax.fori_loop(0, groups, gradients, 0)

    outs = []
    if closes:
        for h in range(n_col // 2):
            for n in range(2):
                at = pl.ds(pl.multiple_of((2 * h + ((col_pos + n) & 1)) * rows, rows), rows)
                if n == 1:
                    src[at] = gs_acc[at].astype(src.dtype)
                outs.append(((src if n else gs_acc).at[at], gs_outs[n].at[h]))
    else:
        outs.append((gs_acc, gs_outs[0]))
    outs = [pltpu.make_async_copy(a, b, sems.at[i]) for i, (a, b) in enumerate(outs)]
    for copy in outs:
        copy.start()
    for i, d in enumerate(parts):
        for n in range(n_x):
            tgt[part_at(d, n)] = gt_acc[part_at(d, n)].astype(tgt.dtype)
            copy = pltpu.make_async_copy(tgt.at[part_at(d, n)], gt_outs[i * n_x + n], sems.at[len(outs)])
            copy.start()
            outs.append(copy)
    for copy in outs:
        copy.wait()


def run_slots(
    first, last, n_col, ratio, scalars, coords, cores, src_parts, tgt_parts, tiles, carried
):
    rows, rank = src_parts[0].shape
    cap, tile = tiles.shape[0], tiles.shape[1]
    n_x, block = last - first, n_col * rows
    any_spec = pl.BlockSpec(memory_space=pl.ANY)
    smem_spec = pl.BlockSpec(memory_space=pltpu.SMEM)
    n_out = len(tgt_parts)
    outs = [jax.ShapeDtypeStruct((rows, rank), jnp.bfloat16)] * n_out
    if last == ratio:
        outs += [jax.ShapeDtypeStruct((n_col // 2, rows, rank), kind) for kind in (jnp.float32, jnp.bfloat16)]
    else:
        outs += [jax.ShapeDtypeStruct((block, rank), jnp.float32)]
    operands = [scalars, coords, cores, *src_parts, *tgt_parts, tiles, *carried]
    outs = pl.pallas_call(
        functools.partial(slots_kernel, first, last, n_col, ratio),
        out_shape=outs,
        in_specs=[smem_spec, smem_spec] + [any_spec] * (len(operands) - 2),
        out_specs=[any_spec] * len(outs),
        scratch_shapes=[
            pltpu.VMEM(cores.shape, cores.dtype),
            pltpu.VMEM((block, rank), jnp.bfloat16),
            pltpu.VMEM((n_x * block, rank), jnp.bfloat16),
            pltpu.VMEM((cap, tile, tile), jnp.bfloat16),
            pltpu.VMEM((cap, tile, tile), jnp.bfloat16),
            pltpu.VMEM((cap, tile, rank), jnp.bfloat16),
            pltpu.VMEM((cap, tile, rank), jnp.bfloat16),
            pltpu.VMEM((block, rank), jnp.float32),
            pltpu.VMEM((n_x * block, rank), jnp.float32),
            pltpu.SMEM((cap + UNROLL,), jnp.int32),
            pltpu.SMEM((cap + UNROLL,), jnp.int32),
            pltpu.SemaphoreType.DMA((cap,)),
            pltpu.SemaphoreType.DMA((2 * n_col * (n_x + 1) + 2,)),
        ],
        compiler_params=pltpu.CompilerParams(vmem_limit_bytes=VMEM_LIMIT),
        cost_estimate=pl.CostEstimate(flops=COST, bytes_accessed=COST, transcendentals=0),
    )(*operands)
    return outs[:n_out], outs[n_out:]


def swap(value, bit, n_col):
    return lax.ppermute(value, "col", [(i, i ^ bit) for i in range(n_col)])


def local(factors, cores, tiles, tile_coords, tile_counts):
    planes = lax.axis_size("zz")
    ratio = lax.axis_size("xx")
    n_col = lax.axis_size("col")
    rows, rank = factors.shape
    tile = tiles.shape[1]
    plane, x_pos, col_pos = lax.axis_index("zz"), lax.axis_index("xx"), lax.axis_index("col")
    scalars = jnp.stack([plane, x_pos, col_pos, tile_counts[0]]).astype(jnp.int32)
    coords = tile_coords.T

    def part_pairs(d, target):
        spots = [(p, x, j) for p in range(planes) for x in range(ratio) for j in range(n_col)]
        at = lambda p, x, j: (p * ratio + x) * n_col + j
        return [(at(p, x, j), at(*target(p, x, j, mirror(p ^ j ^ d, n_col)))) for p, x, j in spots]

    own = {}
    for d in [*range(1, n_col, 2), *range(0, n_col, 2)]:
        pairs = part_pairs(d, lambda p, x, j, q: (j, x, q))
        own[d] = lax.ppermute(factors, AXES, [(b, a) for a, b in pairs])
    src = {0: factors}
    bit = n_col // 2
    while bit:
        for o, value in list(src.items()):
            if bit == 1 and o:
                value = lax.optimization_barrier((value, own[0]))[0]
            src[o | bit] = swap(value, bit, n_col)
        bit //= 2
    src = [src[o] for o in range(n_col)]
    cross = {
        d: [lax.ppermute(own[d], "xx", [(x, (x + s) % ratio) for x in range(ratio)]) for s in range(1, ratio)]
        for d in range(n_col)
    }

    fixed = (n_col, ratio, scalars, coords, cores, src)
    def to_owner(value, d, t):
        return lax.ppermute(value, AXES, part_pairs(d, lambda p, x, j, q: (p, (x - t) % ratio, q)))

    def to_pair(value):
        return lax.ppermute(value, "zz", [(p, p ^ 1) for p in range(planes)])

    halving = [d for d in range(n_col) if d // 2 % 2 == 1]
    direct = [d for d in range(n_col) if d // 2 % 2 == 0]
    own_grad, src_grad = run_slots(0, 1, *fixed, [own[d] for d in range(n_col)], tiles, [])
    came = {d: [to_pair(own_grad[d + 1])] for d in halving[::2]}
    arrived = {d: [to_owner(own_grad[d], d, 0)] for d in direct}
    grads = {d: [own_grad[d]] for d in range(n_col)}
    if ratio > 1:
        held = [v for d in range(n_col) for v in cross[d]]
        target, src_grad = run_slots(1, ratio, *fixed, held, tiles, src_grad)
        target = {d: target[d * (ratio - 1) : (d + 1) * (ratio - 1)] for d in range(n_col)}
        target, came, arrived = lax.optimization_barrier((target, came, arrived))
        for d in range(n_col):
            grads[d].extend(target[d])
        for t in range(1, ratio):
            for d in came:
                came[d].append(to_pair(grads[d + 1][t]))
            for d in direct:
                arrived[d].append(to_owner(grads[d][t], d, t))
    src_keep, src_send = src_grad

    src_sum = src_keep + swap(src_send, 1, n_col).astype(jnp.float32)
    bit = 2
    while bit < n_col:
        pairs = src_sum.reshape(src_sum.shape[0] // 2, 2, rows, rank)
        mine = (col_pos // bit) % 2
        out = lax.dynamic_index_in_dim(pairs, 1 - mine, 1, keepdims=False).astype(jnp.bfloat16)
        kept = lax.dynamic_index_in_dim(pairs, mine, 1, keepdims=False)
        src_sum = kept + swap(out, bit, n_col).astype(jnp.float32)
        bit *= 2
    total = src_sum[0]

    for d in came:
        arrived[d] = [
            to_owner((a.astype(jnp.float32) + b.astype(jnp.float32)).astype(jnp.bfloat16), d, t)
            for t, (a, b) in enumerate(zip(grads[d], came[d]))
        ]
    landed = []
    for d, values in arrived.items():
        term = sum(v.astype(jnp.float32) for v in values).astype(jnp.bfloat16)
        pairs = [
            ((p * ratio + x) * n_col + q, ((p ^ mirror(q, n_col) ^ d) * ratio + x) * n_col + q)
            for p in range(planes)
            for x in range(ratio)
            for q in range(n_col)
        ]
        landed.append(lax.ppermute(term, AXES, pairs))
    total = total + sum(v.astype(jnp.float32) for v in landed)
    return weight_decay * factors.astype(jnp.float32) - total / tile


def solution(mesh):
    n_row, n_col = mesh.shape["row"], mesh.shape["col"]
    split = Mesh(mesh.devices.reshape(n_col, n_row // n_col, n_col), AXES)
    in_specs = (P(AXES, None), P(), P(AXES, None, None), P(AXES, None), P(AXES))
    return jax.shard_map(local, mesh=split, in_specs=in_specs, out_specs=P(AXES, None), check_vma=False)
```

```python
import functools

import jax
import jax.numpy as jnp
from jax import lax
from jax.experimental import pallas as pl
from jax.experimental.pallas import tpu as pltpu
from jax.sharding import Mesh
from jax.sharding import PartitionSpec as P

weight_decay = 1.0
AXES = ("zz", "xx", "col")
UNROLL = 8
VMEM_LIMIT = 56 * 2**20
COST = 0
CONTRACT_LAST = (((1,), (1,)), ((), ()))
CONTRACT_FIRST = (((0,), (0,)), ((), ()))


def dot(a, b, dims=(((1,), (0,)), ((), ()))):
    return lax.dot_general(a, b, dims, preferred_element_type=jnp.float32)


def mirror(value, size):
    out, bit = 0, 1
    while bit < size:
        out = out * 2 + (value // bit) % 2
        bit *= 2
    return out


def slots_kernel(first, last, n_col, ratio, scalars, coords, cores_hbm, *refs):
    n_x = last - first
    opens, closes = first == 0, last == ratio
    parts = [*range(n_col)]
    src_refs, refs = refs[:n_col], refs[n_col:]
    tgt_refs, refs = refs[: len(parts) * n_x], refs[len(parts) * n_x :]
    tiles_hbm, refs = refs[0], refs[1:]
    if not opens:
        gs_in, refs = refs[0], refs[1:]
    gt_outs, refs = refs[: len(parts) * n_x], refs[len(parts) * n_x :]
    gs_outs, refs = (refs[:2], refs[2:]) if closes else (refs[:1], refs[1:])
    cores, src, tgt, tiles, resids, left, right, gs_acc, gt_acc, slot_of, tgt_of, tile_sems, sems = refs
    cap, tile = tiles.shape[0], tiles.shape[1]
    rows = src_refs[0].shape[0]
    src_tiles = n_col * rows // tile
    plane, x_pos, col_pos, live = scalars[0], scalars[1], scalars[2], scalars[3]

    def part_at(d, n):
        place = n * n_col + mirror(plane ^ col_pos ^ d, n_col)
        return pl.ds(pl.multiple_of(place * rows, rows), rows)

    copies = [pltpu.make_async_copy(cores_hbm, cores, sems.at[0])]
    for o in range(n_col):
        at = pl.multiple_of((col_pos ^ o) * rows, rows)
        copies.append(pltpu.make_async_copy(src_refs[o], src.at[pl.ds(at, rows)], sems.at[1 + o]))
    for i, d in enumerate(parts):
        for n in range(n_x):
            index = i * n_x + n
            copies.append(
                pltpu.make_async_copy(tgt_refs[index], tgt.at[part_at(d, n)], sems.at[1 + n_col + index])
            )
    for copy in copies:
        copy.start()
    if not opens:
        gs_copy = pltpu.make_async_copy(gs_in, gs_acc, sems.at[1 + n_col + len(parts) * n_x])
        gs_copy.start()

    def choose(s, count):
        b = coords[2, s]
        step = lax.rem(x_pos - b // src_tiles + ratio, ratio)
        place = lax.rem(b, src_tiles)
        taken = (step >= first) & (step < last)
        slot_of[count] = s
        tgt_of[count] = (step - first) * src_tiles + place

        @pl.when(taken)
        def _():
            pltpu.make_async_copy(tiles_hbm.at[s], tiles.at[count], tile_sems.at[count]).start()

        return count + taken.astype(jnp.int32)

    count = lax.fori_loop(0, live, choose, 0)
    for u in range(UNROLL):
        slot_of[count + u] = 0
        tgt_of[count + u] = 0
    groups = (count + UNROLL - 1) // UNROLL
    if opens:
        gs_acc[...] = jnp.zeros_like(gs_acc)
    gt_acc[...] = jnp.zeros_like(gt_acc)
    for copy in copies:
        copy.wait()

    def place(index):
        return pl.ds(pl.multiple_of(index * tile, tile), tile)

    def products(g, carry):
        for u in range(UNROLL):
            i = g * UNROLL + u
            s = slot_of[i]
            core = cores[coords[0, s]]
            left[i] = dot(src[place(coords[1, s])], core).astype(jnp.bfloat16)
            right[i] = dot(tgt[place(tgt_of[i])], core, CONTRACT_LAST).astype(jnp.bfloat16)
        return carry

    def residuals(g, carry):
        for u in range(UNROLL):
            i = g * UNROLL + u
            predicted = dot(left[i], tgt[place(tgt_of[i])], CONTRACT_LAST)
            resid = jnp.where(i < count, tiles[i].astype(jnp.float32) - predicted, 0.0)
            resids[i] = resid.astype(jnp.bfloat16)
        return carry

    def source_sums(g, carry):
        for u in range(UNROLL):
            i = g * UNROLL + u
            gs_acc[place(coords[1, slot_of[i]])] += dot(resids[i], right[i])
        return carry

    def target_sums(g, carry):
        for u in range(UNROLL):
            i = g * UNROLL + u
            gt_acc[place(tgt_of[i])] += dot(resids[i], left[i], CONTRACT_FIRST)
        return carry

    def arrive(i, carry):
        pltpu.make_async_copy(tiles_hbm.at[slot_of[i]], tiles.at[i], tile_sems.at[i]).wait()
        return carry

    lax.fori_loop(0, groups, products, 0)
    lax.fori_loop(0, count, arrive, 0)
    lax.fori_loop(0, groups, residuals, 0)
    if not opens:
        gs_copy.wait()
    lax.fori_loop(0, groups, source_sums, 0)

    outs = []
    if closes:
        for h in range(n_col // 2):
            for n in range(2):
                at = pl.ds(pl.multiple_of((2 * h + ((col_pos + n) & 1)) * rows, rows), rows)
                if n == 1:
                    src[at] = gs_acc[at].astype(src.dtype)
                outs.append(((src if n else gs_acc).at[at], gs_outs[n].at[h]))
    else:
        outs.append((gs_acc, gs_outs[0]))
    outs = [pltpu.make_async_copy(a, b, sems.at[i]) for i, (a, b) in enumerate(outs)]
    for copy in outs:
        copy.start()
    lax.fori_loop(0, groups, target_sums, 0)
    for i, d in enumerate(parts):
        for n in range(n_x):
            tgt[part_at(d, n)] = gt_acc[part_at(d, n)].astype(tgt.dtype)
            copy = pltpu.make_async_copy(tgt.at[part_at(d, n)], gt_outs[i * n_x + n], sems.at[len(outs)])
            copy.start()
            outs.append(copy)
    for copy in outs:
        copy.wait()


def run_slots(
    first, last, n_col, ratio, scalars, coords, cores, src_parts, tgt_parts, tiles, carried
):
    rows, rank = src_parts[0].shape
    cap, tile = tiles.shape[0], tiles.shape[1]
    n_x, block = last - first, n_col * rows
    any_spec = pl.BlockSpec(memory_space=pl.ANY)
    smem_spec = pl.BlockSpec(memory_space=pltpu.SMEM)
    n_out = len(tgt_parts)
    outs = [jax.ShapeDtypeStruct((rows, rank), jnp.bfloat16)] * n_out
    if last == ratio:
        outs += [jax.ShapeDtypeStruct((n_col // 2, rows, rank), kind) for kind in (jnp.float32, jnp.bfloat16)]
    else:
        outs += [jax.ShapeDtypeStruct((block, rank), jnp.float32)]
    operands = [scalars, coords, cores, *src_parts, *tgt_parts, tiles, *carried]
    outs = pl.pallas_call(
        functools.partial(slots_kernel, first, last, n_col, ratio),
        out_shape=outs,
        in_specs=[smem_spec, smem_spec] + [any_spec] * (len(operands) - 2),
        out_specs=[any_spec] * len(outs),
        scratch_shapes=[
            pltpu.VMEM(cores.shape, cores.dtype),
            pltpu.VMEM((block, rank), jnp.bfloat16),
            pltpu.VMEM((n_x * block, rank), jnp.bfloat16),
            pltpu.VMEM((cap, tile, tile), jnp.bfloat16),
            pltpu.VMEM((cap, tile, tile), jnp.bfloat16),
            pltpu.VMEM((cap, tile, rank), jnp.bfloat16),
            pltpu.VMEM((cap, tile, rank), jnp.bfloat16),
            pltpu.VMEM((block, rank), jnp.float32),
            pltpu.VMEM((n_x * block, rank), jnp.float32),
            pltpu.SMEM((cap + UNROLL,), jnp.int32),
            pltpu.SMEM((cap + UNROLL,), jnp.int32),
            pltpu.SemaphoreType.DMA((cap,)),
            pltpu.SemaphoreType.DMA((2 * n_col * (n_x + 1) + 2,)),
        ],
        compiler_params=pltpu.CompilerParams(vmem_limit_bytes=VMEM_LIMIT),
        cost_estimate=pl.CostEstimate(flops=COST, bytes_accessed=COST, transcendentals=0),
    )(*operands)
    return outs[:n_out], outs[n_out:]


def swap(value, bit, n_col):
    return lax.ppermute(value, "col", [(i, i ^ bit) for i in range(n_col)])


def local(factors, cores, tiles, tile_coords, tile_counts):
    planes = lax.axis_size("zz")
    ratio = lax.axis_size("xx")
    n_col = lax.axis_size("col")
    rows, rank = factors.shape
    tile = tiles.shape[1]
    plane, x_pos, col_pos = lax.axis_index("zz"), lax.axis_index("xx"), lax.axis_index("col")
    scalars = jnp.stack([plane, x_pos, col_pos, tile_counts[0]]).astype(jnp.int32)
    coords = tile_coords.T

    def part_pairs(d, target):
        spots = [(p, x, j) for p in range(planes) for x in range(ratio) for j in range(n_col)]
        at = lambda p, x, j: (p * ratio + x) * n_col + j
        return [(at(p, x, j), at(*target(p, x, j, mirror(p ^ j ^ d, n_col)))) for p, x, j in spots]

    own = {}
    for d in [*range(1, n_col, 2), *range(0, n_col, 2)]:
        pairs = part_pairs(d, lambda p, x, j, q: (j, x, q))
        own[d] = lax.ppermute(factors, AXES, [(b, a) for a, b in pairs])
    src = {0: factors}
    bit = n_col // 2
    while bit:
        for o, value in list(src.items()):
            if bit == 1 and o:
                value = lax.optimization_barrier((value, own[0]))[0]
            src[o | bit] = swap(value, bit, n_col)
        bit //= 2
    src = [src[o] for o in range(n_col)]
    cross = {
        d: [lax.ppermute(own[d], "xx", [(x, (x + s) % ratio) for x in range(ratio)]) for s in range(1, ratio)]
        for d in range(n_col)
    }

    fixed = (n_col, ratio, scalars, coords, cores, src)
    def to_owner(value, d, t):
        return lax.ppermute(value, AXES, part_pairs(d, lambda p, x, j, q: (p, (x - t) % ratio, q)))

    def to_pair(value):
        return lax.ppermute(value, "zz", [(p, p ^ 1) for p in range(planes)])

    halving = [d for d in range(n_col) if d // 2 % 2 == 1]
    direct = [d for d in range(n_col) if d // 2 % 2 == 0]
    own_grad, src_grad = run_slots(0, 1, *fixed, [own[d] for d in range(n_col)], tiles, [])
    came = {d: [to_pair(own_grad[d + 1])] for d in halving[::2]}
    arrived = {d: [to_owner(own_grad[d], d, 0)] for d in direct}
    grads = {d: [own_grad[d]] for d in range(n_col)}
    if ratio > 1:
        held = [v for d in range(n_col) for v in cross[d]]
        target, src_grad = run_slots(1, ratio, *fixed, held, tiles, src_grad)
        target = {d: target[d * (ratio - 1) : (d + 1) * (ratio - 1)] for d in range(n_col)}
        target, came, arrived = lax.optimization_barrier((target, came, arrived))
        for d in range(n_col):
            grads[d].extend(target[d])
        for t in range(1, ratio):
            for d in came:
                came[d].append(to_pair(grads[d + 1][t]))
            for d in direct:
                arrived[d].append(to_owner(grads[d][t], d, t))
    src_keep, src_send = src_grad

    src_sum = src_keep + swap(src_send, 1, n_col).astype(jnp.float32)
    bit = 2
    while bit < n_col:
        pairs = src_sum.reshape(src_sum.shape[0] // 2, 2, rows, rank)
        mine = (col_pos // bit) % 2
        out = lax.dynamic_index_in_dim(pairs, 1 - mine, 1, keepdims=False).astype(jnp.bfloat16)
        kept = lax.dynamic_index_in_dim(pairs, mine, 1, keepdims=False)
        src_sum = kept + swap(out, bit, n_col).astype(jnp.float32)
        bit *= 2
    total = src_sum[0]

    for d in came:
        arrived[d] = [
            to_owner((a.astype(jnp.float32) + b.astype(jnp.float32)).astype(jnp.bfloat16), d, t)
            for t, (a, b) in enumerate(zip(grads[d], came[d]))
        ]
    landed = []
    for d, values in arrived.items():
        term = sum(v.astype(jnp.float32) for v in values).astype(jnp.bfloat16)
        pairs = [
            ((p * ratio + x) * n_col + q, ((p ^ mirror(q, n_col) ^ d) * ratio + x) * n_col + q)
            for p in range(planes)
            for x in range(ratio)
            for q in range(n_col)
        ]
        landed.append(lax.ppermute(term, AXES, pairs))
    total = total + sum(v.astype(jnp.float32) for v in landed)
    return weight_decay * factors.astype(jnp.float32) - total / tile


def solution(mesh):
    n_row, n_col = mesh.shape["row"], mesh.shape["col"]
    split = Mesh(mesh.devices.reshape(n_col, n_row // n_col, n_col), AXES)
    in_specs = (P(AXES, None), P(), P(AXES, None, None), P(AXES, None), P(AXES))
    return jax.shard_map(local, mesh=split, in_specs=in_specs, out_specs=P(AXES, None), check_vma=False)
```
